512 devices in a mesh: inp: 16 (over z), tm: 8 (over y, x_hi), freq: 4 (over x_lo, core).
Axes of the slice: x: 4 (x_hi: 2, x_lo: 2; x = x_hi * 2 + x_lo), y: 4, z: 16, core: 2. Of those that a mesh axis runs over, the one named last changes fastest.
Arguments:
- volt: bfloat16 [2, 32768, 2048], P(None, 'tm', 'inp'), may hold values from -8 to 8
- window: float32 [4, 64], replicated, may hold values from 0.1 to 1
Outputs:
- spectra: bfloat16 [2, 512, 64, 2048], P(None, 'tm', ('freq', 'inp'))
- vis: bfloat16 [2, 64, 2048, 2048], P(None, ('freq', 'inp'), 'tm')
The draws below stay inside these ranges and needn't reach their ends.
All inputs are finite; a program needn't handle non-finite values.
Results may differ from the reference program's by a relative error of at most 0.0034.
Values may be sent and summed in bfloat16 or wider, within the bound.
No kernel may reach another device: no remote copies, remote signals or barrier semaphores. Data moves between devices by JAX's collectives and lax.ppermute only.
A program may use at most 64 MiB of HBM per device.

```python
import math
import jax
import jax.numpy as jnp
from jax import lax

A = 2048
CH = 64
TAPS = 4
FRAMES = 512
SAMPLES = 32768


source_count = 4


def draw_volt(key, part):
    key = jax.random.fold_in(key, 11)
    key_noise, key_signal, key_gain = jax.random.split(key, 3)
    noise = jax.random.normal(key_noise, (2, SAMPLES, A), jnp.float32)
    signal = jax.random.normal(key_signal, (2, source_count, SAMPLES), jnp.float32) * 0.7
    gains = jax.random.normal(key_gain, (2, source_count, A), jnp.float32) * 0.5
    real_part = noise[0]
    imag_part = noise[1]
    for index in range(source_count):
        sr = signal[0, index][:, None]
        si = signal[1, index][:, None]
        gr = gains[0, index][None, :]
        gi = gains[1, index][None, :]
        real_part = real_part + sr * gr - si * gi
        imag_part = imag_part + sr * gi + si * gr
    result = jnp.clip(jnp.stack([real_part, imag_part]), -8.0, 8.0)
    return result.astype(jnp.bfloat16)


def setup_inputs(seed: int = 0) -> dict:
    keys = jax.random.split(jax.random.key(seed), 3)
    volt = draw_volt(jax.random.fold_in(keys[2], 71), 0)
    window = jnp.clip(jax.random.uniform(keys[1], (TAPS, CH), jnp.float32, 0.1, 1.0), 0.1, 1.0)
    return dict(volt=volt, window=window)


def gram(left, right):
    return lax.dot_general(left, right, (((0,), (0,)), ((), ())), preferred_element_type=jnp.float32)

def reference(volt, window):
    series = volt.astype(jnp.float32).reshape(2, FRAMES, CH, A)
    padded = jnp.concatenate([jnp.zeros((2, TAPS - 1, CH, A), jnp.float32), series], axis=1)
    filtered = window[0][None, None, :, None] * padded[:, TAPS - 1:TAPS - 1 + FRAMES]
    for j in range(1, TAPS):
        filtered = filtered + window[j][None, None, :, None] * padded[:, TAPS - 1 - j:TAPS - 1 - j + FRAMES]
    complex_field = jnp.fft.fft(filtered[0] + 1j * filtered[1], axis=1) / math.sqrt(CH)
    spectra = jnp.stack([jnp.real(complex_field), jnp.imag(complex_field)]).astype(jnp.bfloat16)

    def channel_vis(channel):
        chosen = lax.dynamic_index_in_dim(spectra, channel, 2, keepdims=False)
        real_part = gram(chosen[0], chosen[0]) + gram(chosen[1], chosen[1])
        imag_part = gram(chosen[0], chosen[1]) - gram(chosen[1], chosen[0])
        return (jnp.stack([real_part, imag_part]) * (1.0 / FRAMES)).astype(jnp.bfloat16)
    stacked = lax.map(channel_vis, jnp.arange(CH, dtype=jnp.int32))
    return (spectra, jnp.transpose(stacked, (1, 0, 2, 3)))
```

```python
import math

import jax
import jax.numpy as jnp
from jax import lax
from jax.sharding import PartitionSpec as P


def from_behind(value, axis, by):
    count = lax.axis_size(axis)
    pairs = [(i, i + by) for i in range(count) if 0 <= i + by < count]
    return lax.ppermute(value, axis, pairs)


def tm_shift(value, dy, dx):
    ny = lax.axis_size("tm") // 2
    pairs = [
        (y * 2 + h, (y + dy) % ny * 2 + (h + dx) % 2) for y in range(ny) for h in range(2)
    ]
    return lax.ppermute(value, "tm", pairs)


def gather_time(block):
    half = block.shape[1] // 2
    up = tm_shift(block, 1, 0)
    down = tm_shift(block, -1, 0)
    across = tm_shift(block, 0, 1)
    far_a = tm_shift(up[:, :half], 1, 0)
    far_b = tm_shift(down[:, half:], -1, 0)
    far = jnp.concatenate([far_a, far_b], axis=1)
    across_up = tm_shift(across, 1, 0)
    across_down = tm_shift(across, -1, 0)
    across_far = tm_shift(far, 0, 1)
    return [block, up, down, across, far, across_up, across_down, across_far]


def body(volt, window):
    taps, chans = window.shape
    samples = volt.shape[1]
    width = volt.shape[2]
    frames = samples // chans
    series = volt.reshape(2, frames, chans, width)
    tail = series[:, frames - (taps - 1) :]
    prior = from_behind(tail, "tm", 1)
    extended = jnp.concatenate([prior, series], axis=1)
    filtered = window[0][None, None, :, None] * extended[:, taps - 1 : taps - 1 + frames]
    for j in range(1, taps):
        filtered = (
            filtered
            + window[j][None, None, :, None] * extended[:, taps - 1 - j : taps - 1 - j + frames]
        )
    group_size = chans // lax.axis_size("freq")
    channel_ids = lax.axis_index("freq") * group_size + jnp.arange(group_size, dtype=jnp.int32)
    positions = jnp.arange(chans, dtype=jnp.int32)
    phase = (positions[:, None] * channel_ids[None, :] % chans).astype(jnp.float32) * (
        2.0 * math.pi / chans
    )
    norm_factor = 1.0 / math.sqrt(chans)
    cosine = jnp.cos(phase) * norm_factor
    sine = jnp.sin(phase) * norm_factor
    table = jnp.stack([jnp.stack([cosine, -sine], axis=1), jnp.stack([sine, cosine], axis=1)])
    channelized = jnp.einsum(
        "pfka,pkqc->qfca",
        filtered,
        table,
        precision=lax.Precision.HIGHEST,
        preferred_element_type=jnp.float32,
    )
    local_spectra = channelized.astype(jnp.bfloat16)
    turned = lax.all_to_all(local_spectra, "inp", split_axis=2, concat_axis=3, tiled=True)
    blocks = lax.axis_size("tm")
    inputs = turned.shape[3]
    block_rows = inputs // blocks
    own_block = lax.axis_index("tm")
    scale = 1.0 / (frames * blocks)
    pieces = gather_time(turned[:, :, 0])
    columns = jnp.concatenate([p.reshape(2 * frames, inputs) for p in pieces], axis=0)
    rows = lax.dynamic_slice_in_dim(columns, own_block * block_rows, block_rows, 1)
    rows = rows.reshape(blocks, 2, frames, block_rows)
    turned_rows = jnp.stack([-rows[:, 1], rows[:, 0]], axis=1)
    left = jnp.concatenate([rows, turned_rows], axis=3).reshape(blocks * 2 * frames, 2 * block_rows)
    product = lax.dot_general(
        left, columns, (((0,), (0,)), ((), ())), preferred_element_type=jnp.float32
    )
    vis = (product * scale).astype(jnp.bfloat16).reshape(2, 1, block_rows, inputs)
    return (turned, vis)


def solution(mesh):
    in_specs = (P(None, "tm", "inp"), P())
    out_specs = (P(None, "tm", ("freq", "inp"), None), P(None, ("freq", "inp"), "tm", None))
    return jax.shard_map(body, mesh=mesh, in_specs=in_specs, out_specs=out_specs, check_vma=False)
```

```python
import functools
import math

import jax
import jax.numpy as jnp
import numpy as np
from jax import lax
from jax.experimental import pallas as pl
from jax.experimental.pallas import tpu as pltpu
from jax.sharding import PartitionSpec as P

VM = pl.BlockSpec(memory_space=pltpu.VMEM)
SM = pl.BlockSpec(memory_space=pltpu.SMEM)
HB = pl.BlockSpec(memory_space=pltpu.HBM)
LOAD_LIMIT = 50 << 20
PARAMS = pltpu.CompilerParams(vmem_limit_bytes=16 << 20)


def from_behind(value, axis, by):
    count = lax.axis_size(axis)
    pairs = [(i, i + by) for i in range(count) if 0 <= i + by < count]
    return lax.ppermute(value, axis, pairs)


def tm_shift(value, dy, dx):
    ny = lax.axis_size("tm") // 2
    pairs = [
        (y * 2 + h, (y + dy) % ny * 2 + (h + dx) % 2) for y in range(ny) for h in range(2)
    ]
    return lax.ppermute(value, "tm", pairs)


def shares_of(taps, table_ref, frames):
    rows = table_ref.shape[0] // (2 * taps)
    width = frames[0][0].shape[1]
    x = jnp.concatenate([jnp.concatenate([p[0], p[1]], axis=0) for p in frames], axis=1)
    y = jnp.dot(table_ref[...], x, preferred_element_type=jnp.float32)
    parts = []
    for j in range(taps):
        at = 2 * j * rows
        parts.append(y[at : at + rows] + y[at + rows : at + 2 * rows])
    return [[part[:, s * width : (s + 1) * width] for part in parts] for s in range(len(frames))]


def advance(carry, share):
    sums = [c + s for c, s in zip(carry, share)] + [share[-1]]
    return sums[0], tuple(sums[1:])


def load_kernel(volt_ref, tail_ref, held_ref, sems):
    chunks = sems.shape[0] - 1
    samples = volt_ref.shape[1]
    span = samples // chunks
    last = tail_ref.shape[1]
    copies = [pltpu.make_async_copy(volt_ref.at[:, samples - last :], tail_ref, sems.at[chunks])]
    for i in range(chunks):
        part = slice(i * span, (i + 1) * span)
        copies.append(pltpu.make_async_copy(volt_ref.at[:, part], held_ref.at[:, part], sems.at[i]))
    for copy in copies:
        copy.start()
    for copy in copies:
        copy.wait()


def load(volt, last):
    return pl.pallas_call(
        load_kernel,
        out_shape=(
            jax.ShapeDtypeStruct((volt.shape[0], last, volt.shape[2]), volt.dtype),
            jax.ShapeDtypeStruct(volt.shape, volt.dtype),
        ),
        in_specs=[HB],
        out_specs=(VM, VM),
        scratch_shapes=[pltpu.SemaphoreType.DMA((5,))],
        cost_estimate=pl.CostEstimate(flops=0, bytes_accessed=4 * volt.size, transcendentals=0),
        compiler_params=pltpu.CompilerParams(vmem_limit_bytes=LOAD_LIMIT),
        name="load",
    )(volt)


def main_kernel(taps, _, table_ref, window_ref, volt_ref, out_ref, open_ref, split_ref):
    frames, rows, width = out_ref.shape
    chans = volt_ref.shape[1] // frames
    halo = taps - 1
    step = 8

    def frame_of(f):
        at = f * chans if isinstance(f, int) else pl.multiple_of(f * chans, chans)
        return [volt_ref[p, pl.ds(at, chans), :] for p in range(2)]

    base = table_ref[...]
    for j in range(taps):
        weights = window_ref[j : j + 1, :]
        tapped = base * jnp.concatenate([weights, weights], axis=1)
        coarse = tapped.astype(jnp.bfloat16)
        at = 2 * j * rows
        split_ref[at : at + rows, :] = coarse
        split_ref[at + rows : at + 2 * rows, :] = (tapped - coarse.astype(jnp.float32)).astype(jnp.bfloat16)

    def block(i, carry):
        every = []
        for s in range(0, step, 2):
            every += shares_of(taps, split_ref, [frame_of(i * step + s), frame_of(i * step + s + 1)])
        for s, share in enumerate(every):
            done, carry = advance(carry, share)
            out_ref[i * step + s] = done.astype(out_ref.dtype)
            if isinstance(i, int) and s < halo:
                open_ref[s] = done
        return carry

    carry = block(0, tuple(jnp.zeros((rows, width), jnp.float32) for _ in range(halo)))
    lax.fori_loop(1, frames // step, block, carry)


def head_kernel(taps, table_ref, prior_ref, open_ref, main_ref, out_ref):
    rows, width = out_ref.shape[1:]
    halo = taps - 1
    chans = prior_ref.shape[1] // halo
    frames = [[prior_ref[p, f * chans : (f + 1) * chans, :] for p in range(2)] for f in range(halo)]
    carry = tuple(jnp.zeros((rows, width), jnp.float32) for _ in range(halo))
    for share in shares_of(taps, table_ref, frames):
        _, carry = advance(carry, share)
    for f in range(halo):
        out_ref[f] = (open_ref[f] + carry[f]).astype(out_ref.dtype)


def dft_table(chans, group_size):
    channel = np.arange(chans).reshape(-1, group_size)
    phase = channel[:, :, None] * np.arange(chans) % chans * (2.0 * math.pi / chans)
    cosine = np.cos(phase) / math.sqrt(chans)
    sine = np.sin(phase) / math.sqrt(chans)
    real = np.concatenate([cosine, sine], axis=2)
    imag = np.concatenate([-sine, cosine], axis=2)
    return np.concatenate([real, imag], axis=1).astype(np.float32)


def channelize(held, prior, window, group, groups, frames):
    taps, chans = window.shape
    rows = 2 * chans // groups
    width = held.shape[2]
    table = jnp.asarray(dft_table(chans, chans // groups))
    local, open_sums, split = pl.pallas_call(
        functools.partial(main_kernel, taps),
        out_shape=(
            jax.ShapeDtypeStruct((frames, rows, width), jnp.bfloat16),
            jax.ShapeDtypeStruct((taps - 1, rows, width), jnp.float32),
            jax.ShapeDtypeStruct((taps * 2 * rows, 2 * chans), jnp.bfloat16),
        ),
        grid_spec=pltpu.PrefetchScalarGridSpec(
            num_scalar_prefetch=1,
            grid=(1,),
            in_specs=[
                pl.BlockSpec((None, rows, 2 * chans), lambda i, group: (group[0], 0, 0)),
                VM,
                VM,
            ],
            out_specs=(VM, VM, VM),
        ),
        cost_estimate=pl.CostEstimate(
            flops=4 * rows * taps * held.size, bytes_accessed=3 * held.size, transcendentals=0
        ),
        compiler_params=PARAMS,
        name="channelize",
    )(group, table, window, held)
    return pl.pallas_call(
        functools.partial(head_kernel, taps),
        out_shape=jax.ShapeDtypeStruct(local.shape, local.dtype),
        in_specs=[VM] * 4,
        out_specs=VM,
        input_output_aliases={3: 0},
        cost_estimate=pl.CostEstimate(
            flops=4 * rows * taps * prior.size, bytes_accessed=3 * prior.size, transcendentals=0
        ),
        compiler_params=PARAMS,
        name="channelize_head",
    )(split, prior, open_sums, local)


def fill_left(left_ref, at, piece, first, parts):
    blocks = [piece[first + s] for s in range(parts)]
    rows = jnp.concatenate([jnp.concatenate([b[0], b[1]], axis=0) for b in blocks], axis=1)
    turned = jnp.concatenate([jnp.concatenate([-b[1], b[0]], axis=0) for b in blocks], axis=1)
    both = jnp.concatenate([rows, turned], axis=1)
    left_ref[:, at : at + both.shape[0]] = both.T


def column_tile(pieces, z, wide):
    tall = []
    for piece in pieces:
        across = [piece[z + s] for s in range(wide)]
        across = [jnp.concatenate([b[0], b[1]], axis=0) for b in across]
        tall.append(jnp.concatenate(across, axis=1))
    return jnp.concatenate(tall, axis=0)


def spectra_kernel(block_ref, spectra_ref, token_ref, sems):
    token_ref[...] = jnp.zeros_like(token_ref)
    zs, _, _, width = block_ref.shape
    copies = []
    for z in range(zs):
        cols = slice(z * width, (z + 1) * width)
        copies.append(pltpu.make_async_copy(block_ref.at[z], spectra_ref.at[:, :, cols], sems.at[z]))
        copies[-1].start()
    for copy in copies:
        copy.wait()


def first_kernel(wide, own_ref, *refs):
    *pieces, total_ref, left_ref = refs
    zs, _, frames, width = pieces[0].shape
    parts = left_ref.shape[0] // (2 * width)
    for i, piece in enumerate(pieces):
        fill_left(left_ref, 2 * frames * i, piece, own_ref[0] * parts, parts)
    for z in range(0, zs, wide):
        total_ref[:, z * width : (z + wide) * width] = jnp.dot(
            left_ref[...], column_tile(pieces, z, wide), preferred_element_type=jnp.float32
        )


def more_kernel(wide, own_ref, before_ref, *refs):
    *pieces, total_ref, left_ref = refs
    zs, _, frames, width = pieces[0].shape
    parts = left_ref.shape[0] // (2 * width)
    for i, piece in enumerate(pieces):
        fill_left(left_ref, 2 * frames * i, piece, own_ref[0] * parts, parts)
    for z in range(0, zs, wide):
        cols = slice(z * width, (z + wide) * width)
        total_ref[:, cols] = before_ref[:, cols] + jnp.dot(
            left_ref[...], column_tile(pieces, z, wide), preferred_element_type=jnp.float32
        )


def last_kernel(wide, scale, own_ref, total_ref, low_ref, high_ref, vis_ref, left_ref, out_ref, sems):
    cut, _, frames, width = low_ref.shape
    zs = cut + high_ref.shape[0]
    rows = out_ref.shape[1]
    parts = rows // width
    first = own_ref[0] * parts

    @pl.when(first < cut)
    def _():
        fill_left(left_ref, 0, low_ref, first, parts)

    @pl.when(first >= cut)
    def _():
        fill_left(left_ref, 0, high_ref, first - cut, parts)

    copies = []
    for i, z in enumerate(range(0, zs, wide)):
        piece, at = (low_ref, z) if z < cut else (high_ref, z - cut)
        cols = slice(z * width, (z + wide) * width)
        product = jnp.dot(
            left_ref[...], column_tile([piece], at, wide), preferred_element_type=jnp.float32
        )
        out = ((product + total_ref[:, cols]) * scale).astype(out_ref.dtype)
        out_ref[0, :, cols] = out[:rows]
        out_ref[1, :, cols] = out[rows:]
        copies.append(
            pltpu.make_async_copy(out_ref.at[:, :, cols], vis_ref.at[:, :, cols], sems.at[i])
        )
        copies[-1].start()
    for copy in copies:
        copy.wait()


def spectra_of(block):
    zs, _, frames, width = block.shape
    return pl.pallas_call(
        spectra_kernel,
        out_shape=(
            jax.ShapeDtypeStruct((2, frames, zs * width), jnp.bfloat16),
            jax.ShapeDtypeStruct((8, 128), jnp.float32),
        ),
        in_specs=[VM],
        out_specs=(HB, VM),
        scratch_shapes=[pltpu.SemaphoreType.DMA((zs,))],
        cost_estimate=pl.CostEstimate(flops=0, bytes_accessed=4 * block.size, transcendentals=0),
        compiler_params=PARAMS,
        name="spectra_out",
    )(block)


def vis_first(own, pieces, rows):
    zs, _, frames, width = pieces[0].shape
    cols = zs * width
    depth = 2 * frames * len(pieces)
    return pl.pallas_call(
        functools.partial(first_kernel, 2),
        out_shape=jax.ShapeDtypeStruct((2 * rows, cols), jnp.float32),
        in_specs=[SM] + [VM] * len(pieces),
        out_specs=VM,
        scratch_shapes=[pltpu.VMEM((2 * rows, depth), jnp.bfloat16)],
        cost_estimate=pl.CostEstimate(
            flops=4 * rows * cols * depth, bytes_accessed=8 * rows * cols, transcendentals=0
        ),
        compiler_params=PARAMS,
        name="vis_first",
    )(own, *pieces)


def vis_more(own, total, pieces, rows):
    zs, _, frames, width = pieces[0].shape
    cols = zs * width
    depth = 2 * frames * len(pieces)
    return pl.pallas_call(
        functools.partial(more_kernel, 2),
        out_shape=jax.ShapeDtypeStruct((2 * rows, cols), jnp.float32),
        in_specs=[SM, VM] + [VM] * len(pieces),
        out_specs=VM,
        scratch_shapes=[pltpu.VMEM((2 * rows, depth), jnp.bfloat16)],
        input_output_aliases={1: 0},
        cost_estimate=pl.CostEstimate(
            flops=4 * rows * cols * depth, bytes_accessed=8 * rows * cols, transcendentals=0
        ),
        compiler_params=PARAMS,
        name="vis_more",
    )(own, total, *pieces)


def vis_last(own, total, low, high, rows, scale):
    frames, width = low.shape[2:]
    zs = low.shape[0] + high.shape[0]
    cols = zs * width
    wide = 2
    return pl.pallas_call(
        functools.partial(last_kernel, wide, scale),
        out_shape=jax.ShapeDtypeStruct((2, rows, cols), jnp.bfloat16),
        in_specs=[SM, VM, VM, VM],
        out_specs=HB,
        scratch_shapes=[
            pltpu.VMEM((2 * rows, 2 * frames), jnp.bfloat16),
            pltpu.VMEM((2, rows, cols), jnp.bfloat16),
            pltpu.SemaphoreType.DMA((zs // wide,)),
        ],
        cost_estimate=pl.CostEstimate(
            flops=8 * rows * cols * frames, bytes_accessed=8 * rows * cols, transcendentals=0
        ),
        compiler_params=PARAMS,
        name="vis_last",
    )(own, total, low, high)


def after_kernel(*refs):
    pass


def after(other, *values):
    count = len(values)
    return pl.pallas_call(
        after_kernel,
        out_shape=tuple(jax.ShapeDtypeStruct(v.shape, v.dtype) for v in values),
        in_specs=[VM] * count + [pl.BlockSpec(memory_space=pl.ANY)],
        out_specs=(VM,) * count,
        input_output_aliases={i: i for i in range(count)},
        compiler_params=PARAMS,
        name="after",
    )(*values, other)


def correlate(block, own, rows, scale):
    cut = block.shape[0] * 5 // 16 * 2
    up = tm_shift(block, 1, 0)
    across = tm_shift(block, 0, 1)
    down = tm_shift(block, -1, 0)
    spectra, written = spectra_of(block)
    (up,) = after(written, up)
    far = tm_shift(up, 1, 0)
    across_up = tm_shift(up, 0, 1)
    across, down = after(written, across, down)
    across_down = tm_shift(across, -1, 0)
    total = vis_first(own, [block, up, across, down], rows)
    (far,) = after(total, far)
    last_low = tm_shift(far[:cut], 0, 1)
    last_high = tm_shift(across_up[cut:], 1, 0)
    total = vis_more(own, total, [far, across_up, across_down], rows)
    return spectra, vis_last(own, total, last_low, last_high, rows, scale)


def body(volt, window):
    taps, chans = window.shape
    samples, width = volt.shape[1:]
    frames = samples // chans
    tail, held = load(volt, (taps - 1) * chans)
    prior = from_behind(tail, "tm", 1)
    groups = lax.axis_size("freq")
    group = lax.axis_index("freq").astype(jnp.int32).reshape(1)
    local = channelize(held, prior, window, group, groups, frames)
    local = jnp.transpose(local.reshape(frames, 2, chans // groups, width), (2, 1, 0, 3))
    block = lax.all_to_all(local, "inp", split_axis=0, concat_axis=0, tiled=True)
    inputs = block.shape[0] * width
    blocks = lax.axis_size("tm")
    own = lax.axis_index("tm").astype(jnp.int32).reshape(1)
    spectra, vis = correlate(block, own, inputs // blocks, 1.0 / (frames * blocks))
    return (spectra[:, :, None], vis[:, None])


def solution(mesh):
    in_specs = (P(None, "tm", "inp"), P())
    out_specs = (P(None, "tm", ("freq", "inp"), None), P(None, ("freq", "inp"), "tm", None))
    return jax.shard_map(body, mesh=mesh, in_specs=in_specs, out_specs=out_specs, check_vma=False)
```

```python
import functools
import math

import jax
import jax.numpy as jnp
import numpy as np
from jax import lax
from jax.experimental import pallas as pl
from jax.experimental.pallas import tpu as pltpu
from jax.sharding import PartitionSpec as P

VM = pl.BlockSpec(memory_space=pltpu.VMEM)
SM = pl.BlockSpec(memory_space=pltpu.SMEM)
HB = pl.BlockSpec(memory_space=pltpu.HBM)
LOAD_LIMIT = 50 << 20
PARAMS = pltpu.CompilerParams(vmem_limit_bytes=16 << 20)


def from_behind(value):
    count, groups = lax.axis_size("tm"), lax.axis_size("freq")
    pairs = [
        (t * groups + (f ^ (groups // 2)), (t + 1) * groups + f)
        for t in range(count - 1)
        for f in range(groups)
    ]
    return lax.ppermute(value, ("tm", "freq"), pairs)


def tm_shift(value, dy, dx):
    ny = lax.axis_size("tm") // 2
    pairs = [
        (y * 2 + h, (y - dy) % ny * 2 + (h + dx) % 2) for y in range(ny) for h in range(2)
    ]
    return lax.ppermute(value, "tm", pairs)


def shares_of(taps, table_ref, frames):
    rows = table_ref.shape[0] // (2 * taps)
    width = frames[0][0].shape[1]
    x = jnp.concatenate([jnp.concatenate([p[0], p[1]], axis=0) for p in frames], axis=1)
    y = jnp.dot(table_ref[...], x, preferred_element_type=jnp.float32)
    parts = []
    for j in range(taps):
        at = 2 * j * rows
        parts.append(y[at : at + rows] + y[at + rows : at + 2 * rows])
    return [[part[:, s * width : (s + 1) * width] for part in parts] for s in range(len(frames))]


def advance(carry, share):
    sums = [c + s for c, s in zip(carry, share)] + [share[-1]]
    return sums[0], tuple(sums[1:])


def load_kernel(volt_ref, tail_ref, held_ref, sems):
    chunks = sems.shape[0] - 1
    samples = volt_ref.shape[1]
    span = samples // chunks
    last = tail_ref.shape[1]
    copies = [pltpu.make_async_copy(volt_ref.at[:, samples - last :], tail_ref, sems.at[chunks])]
    for i in range(chunks):
        part = slice(i * span, (i + 1) * span)
        copies.append(pltpu.make_async_copy(volt_ref.at[:, part], held_ref.at[:, part], sems.at[i]))
    for copy in copies:
        copy.start()
    for copy in copies:
        copy.wait()


def load(volt, last):
    return pl.pallas_call(
        load_kernel,
        out_shape=(
            jax.ShapeDtypeStruct((volt.shape[0], last, volt.shape[2]), volt.dtype),
            jax.ShapeDtypeStruct(volt.shape, volt.dtype),
        ),
        in_specs=[HB],
        out_specs=(VM, VM),
        scratch_shapes=[pltpu.SemaphoreType.DMA((5,))],
        cost_estimate=pl.CostEstimate(flops=0, bytes_accessed=4 * volt.size, transcendentals=0),
        compiler_params=pltpu.CompilerParams(vmem_limit_bytes=LOAD_LIMIT),
        name="load",
    )(volt)


def main_kernel(taps, _, table_ref, window_ref, volt_ref, out_ref, open_ref, split_ref):
    frames, rows, width = out_ref.shape
    chans = volt_ref.shape[1] // frames
    halo = taps - 1
    step = 8

    def frame_of(f):
        at = f * chans if isinstance(f, int) else pl.multiple_of(f * chans, chans)
        return [volt_ref[p, pl.ds(at, chans), :] for p in range(2)]

    base = table_ref[...]
    for j in range(taps):
        weights = window_ref[j : j + 1, :]
        tapped = base * jnp.concatenate([weights, weights], axis=1)
        coarse = tapped.astype(jnp.bfloat16)
        at = 2 * j * rows
        split_ref[at : at + rows, :] = coarse
        split_ref[at + rows : at + 2 * rows, :] = (tapped - coarse.astype(jnp.float32)).astype(jnp.bfloat16)

    def block(i, carry):
        every = []
        for s in range(0, step, 2):
            every += shares_of(taps, split_ref, [frame_of(i * step + s), frame_of(i * step + s + 1)])
        for s, share in enumerate(every):
            done, carry = advance(carry, share)
            out_ref[i * step + s] = done.astype(out_ref.dtype)
            if isinstance(i, int) and s < halo:
                open_ref[s] = done
        return carry

    carry = block(0, tuple(jnp.zeros((rows, width), jnp.float32) for _ in range(halo)))
    lax.fori_loop(1, frames // step, block, carry)


def head_kernel(taps, table_ref, prior_ref, open_ref, main_ref, out_ref):
    rows, width = out_ref.shape[1:]
    halo = taps - 1
    chans = prior_ref.shape[1] // halo
    frames = [[prior_ref[p, f * chans : (f + 1) * chans, :] for p in range(2)] for f in range(halo)]
    carry = tuple(jnp.zeros((rows, width), jnp.float32) for _ in range(halo))
    for share in shares_of(taps, table_ref, frames):
        _, carry = advance(carry, share)
    for f in range(halo):
        out_ref[f] = (open_ref[f] + carry[f]).astype(out_ref.dtype)


def dft_table(chans, group_size):
    channel = np.arange(chans).reshape(-1, group_size)
    phase = channel[:, :, None] * np.arange(chans) % chans * (2.0 * math.pi / chans)
    cosine = np.cos(phase) / math.sqrt(chans)
    sine = np.sin(phase) / math.sqrt(chans)
    real = np.concatenate([cosine, sine], axis=2)
    imag = np.concatenate([-sine, cosine], axis=2)
    return np.concatenate([real, imag], axis=1).astype(np.float32)


def channelize(held, prior, window, group, groups, frames):
    taps, chans = window.shape
    rows = 2 * chans // groups
    width = held.shape[2]
    table = jnp.asarray(dft_table(chans, chans // groups))
    local, open_sums, split = pl.pallas_call(
        functools.partial(main_kernel, taps),
        out_shape=(
            jax.ShapeDtypeStruct((frames, rows, width), jnp.bfloat16),
            jax.ShapeDtypeStruct((taps - 1, rows, width), jnp.float32),
            jax.ShapeDtypeStruct((taps * 2 * rows, 2 * chans), jnp.bfloat16),
        ),
        grid_spec=pltpu.PrefetchScalarGridSpec(
            num_scalar_prefetch=1,
            grid=(1,),
            in_specs=[
                pl.BlockSpec((None, rows, 2 * chans), lambda i, group: (group[0], 0, 0)),
                VM,
                VM,
            ],
            out_specs=(VM, VM, VM),
        ),
        cost_estimate=pl.CostEstimate(
            flops=4 * rows * taps * held.size, bytes_accessed=3 * held.size, transcendentals=0
        ),
        compiler_params=PARAMS,
        name="channelize",
    )(group, table, window, held)
    return pl.pallas_call(
        functools.partial(head_kernel, taps),
        out_shape=jax.ShapeDtypeStruct(local.shape, local.dtype),
        in_specs=[VM] * 4,
        out_specs=VM,
        input_output_aliases={3: 0},
        cost_estimate=pl.CostEstimate(
            flops=4 * rows * taps * prior.size, bytes_accessed=3 * prior.size, transcendentals=0
        ),
        compiler_params=PARAMS,
        name="channelize_head",
    )(split, prior, open_sums, local)


def fill_left(left_ref, at, piece, first, parts):
    blocks = [piece[first + s] for s in range(parts)]
    rows = jnp.concatenate([jnp.concatenate([b[0], b[1]], axis=0) for b in blocks], axis=1)
    turned = jnp.concatenate([jnp.concatenate([-b[1], b[0]], axis=0) for b in blocks], axis=1)
    both = jnp.concatenate([rows, turned], axis=1)
    left_ref[:, at : at + both.shape[0]] = both.T


def column_tile(pieces, z, wide):
    tall = []
    for piece in pieces:
        across = [piece[z + s] for s in range(wide)]
        across = [jnp.concatenate([b[0], b[1]], axis=0) for b in across]
        tall.append(jnp.concatenate(across, axis=1))
    return jnp.concatenate(tall, axis=0)


def spectra_kernel(block_ref, spectra_ref, token_ref, sems):
    token_ref[...] = jnp.zeros_like(token_ref)
    zs, _, _, width = block_ref.shape
    copies = []
    for z in range(zs):
        cols = slice(z * width, (z + 1) * width)
        copies.append(pltpu.make_async_copy(block_ref.at[z], spectra_ref.at[:, :, cols], sems.at[z]))
        copies[-1].start()
    for copy in copies:
        copy.wait()


def first_kernel(wide, own_ref, *refs):
    *pieces, total_ref, left_ref = refs
    zs, _, frames, width = pieces[0].shape
    parts = left_ref.shape[0] // (2 * width)
    for i, piece in enumerate(pieces):
        fill_left(left_ref, 2 * frames * i, piece, own_ref[0] * parts, parts)
    for z in range(0, zs, wide):
        total_ref[:, z * width : (z + wide) * width] = jnp.dot(
            left_ref[...], column_tile(pieces, z, wide), preferred_element_type=jnp.float32
        )


def more_kernel(wide, own_ref, before_ref, *refs):
    *pieces, total_ref, left_ref = refs
    zs, _, frames, width = pieces[0].shape
    parts = left_ref.shape[0] // (2 * width)
    for i, piece in enumerate(pieces):
        fill_left(left_ref, 2 * frames * i, piece, own_ref[0] * parts, parts)
    for z in range(0, zs, wide):
        cols = slice(z * width, (z + wide) * width)
        total_ref[:, cols] = before_ref[:, cols] + jnp.dot(
            left_ref[...], column_tile(pieces, z, wide), preferred_element_type=jnp.float32
        )


def last_kernel(wide, scale, own_ref, total_ref, low_ref, high_ref, vis_ref, left_ref, out_ref, sems):
    cut, _, frames, width = low_ref.shape
    zs = cut + high_ref.shape[0]
    rows = out_ref.shape[1]
    parts = rows // width
    first = own_ref[0] * parts

    @pl.when(first < cut)
    def _():
        fill_left(left_ref, 0, low_ref, first, parts)

    @pl.when(first >= cut)
    def _():
        fill_left(left_ref, 0, high_ref, first - cut, parts)

    copies = []
    for i, z in enumerate(range(0, zs, wide)):
        piece, at = (low_ref, z) if z < cut else (high_ref, z - cut)
        cols = slice(z * width, (z + wide) * width)
        product = jnp.dot(
            left_ref[...], column_tile([piece], at, wide), preferred_element_type=jnp.float32
        )
        out = ((product + total_ref[:, cols]) * scale).astype(out_ref.dtype)
        out_ref[0, :, cols] = out[:rows]
        out_ref[1, :, cols] = out[rows:]
        copies.append(
            pltpu.make_async_copy(out_ref.at[:, :, cols], vis_ref.at[:, :, cols], sems.at[i])
        )
        copies[-1].start()
    for copy in copies:
        copy.wait()


def spectra_of(block):
    zs, _, frames, width = block.shape
    return pl.pallas_call(
        spectra_kernel,
        out_shape=(
            jax.ShapeDtypeStruct((2, frames, zs * width), jnp.bfloat16),
            jax.ShapeDtypeStruct((8, 128), jnp.float32),
        ),
        in_specs=[VM],
        out_specs=(HB, VM),
        scratch_shapes=[pltpu.SemaphoreType.DMA((zs,))],
        cost_estimate=pl.CostEstimate(flops=0, bytes_accessed=4 * block.size, transcendentals=0),
        compiler_params=PARAMS,
        name="spectra_out",
    )(block)


def vis_first(own, pieces, rows):
    zs, _, frames, width = pieces[0].shape
    cols = zs * width
    depth = 2 * frames * len(pieces)
    return pl.pallas_call(
        functools.partial(first_kernel, 2),
        out_shape=jax.ShapeDtypeStruct((2 * rows, cols), jnp.float32),
        in_specs=[SM] + [VM] * len(pieces),
        out_specs=VM,
        scratch_shapes=[pltpu.VMEM((2 * rows, depth), jnp.bfloat16)],
        cost_estimate=pl.CostEstimate(
            flops=4 * rows * cols * depth, bytes_accessed=8 * rows * cols, transcendentals=0
        ),
        compiler_params=PARAMS,
        name="vis_first",
    )(own, *pieces)


def vis_more(own, total, pieces, rows):
    zs, _, frames, width = pieces[0].shape
    cols = zs * width
    depth = 2 * frames * len(pieces)
    return pl.pallas_call(
        functools.partial(more_kernel, 2),
        out_shape=jax.ShapeDtypeStruct((2 * rows, cols), jnp.float32),
        in_specs=[SM, VM] + [VM] * len(pieces),
        out_specs=VM,
        scratch_shapes=[pltpu.VMEM((2 * rows, depth), jnp.bfloat16)],
        input_output_aliases={1: 0},
        cost_estimate=pl.CostEstimate(
            flops=4 * rows * cols * depth, bytes_accessed=8 * rows * cols, transcendentals=0
        ),
        compiler_params=PARAMS,
        name="vis_more",
    )(own, total, *pieces)


def vis_last(own, total, low, high, rows, scale):
    frames, width = low.shape[2:]
    zs = low.shape[0] + high.shape[0]
    cols = zs * width
    wide = 2
    return pl.pallas_call(
        functools.partial(last_kernel, wide, scale),
        out_shape=jax.ShapeDtypeStruct((2, rows, cols), jnp.bfloat16),
        in_specs=[SM, VM, VM, VM],
        out_specs=HB,
        scratch_shapes=[
            pltpu.VMEM((2 * rows, 2 * frames), jnp.bfloat16),
            pltpu.VMEM((2, rows, cols), jnp.bfloat16),
            pltpu.SemaphoreType.DMA((zs // wide,)),
        ],
        cost_estimate=pl.CostEstimate(
            flops=8 * rows * cols * frames, bytes_accessed=8 * rows * cols, transcendentals=0
        ),
        compiler_params=PARAMS,
        name="vis_last",
    )(own, total, low, high)


def after_kernel(*refs):
    pass


def after(other, *values):
    count = len(values)
    return pl.pallas_call(
        after_kernel,
        out_shape=tuple(jax.ShapeDtypeStruct(v.shape, v.dtype) for v in values),
        in_specs=[VM] * count + [pl.BlockSpec(memory_space=pl.ANY)],
        out_specs=(VM,) * count,
        input_output_aliases={i: i for i in range(count)},
        compiler_params=PARAMS,
        name="after",
    )(*values, other)


def correlate(block, own, rows, scale):
    cut = block.shape[0] * 4 // 16 * 2
    up = tm_shift(block, 1, 0)
    across = tm_shift(block, 0, 1)
    down = tm_shift(block, -1, 0)
    spectra, written = spectra_of(block)
    (up,) = after(written, up)
    far = tm_shift(up, 1, 0)
    across_up = tm_shift(up, 0, 1)
    across, down = after(written, across, down)
    across_down = tm_shift(across, -1, 0)
    total = vis_first(own, [block, up, across, down], rows)
    (far,) = after(total, far)
    last_low = tm_shift(far[:cut], 0, 1)
    last_high = tm_shift(across_up[cut:], 1, 0)
    total = vis_more(own, total, [far, across_up, across_down], rows)
    return spectra, vis_last(own, total, last_low, last_high, rows, scale)


def body(volt, window):
    taps, chans = window.shape
    samples, width = volt.shape[1:]
    frames = samples // chans
    tail, held = load(volt, (taps - 1) * chans)
    prior = from_behind(tail)
    groups = lax.axis_size("freq")
    group = lax.axis_index("freq").astype(jnp.int32).reshape(1)
    local = channelize(held, prior, window, group, groups, frames)
    local = jnp.transpose(local.reshape(frames, 2, chans // groups, width), (2, 1, 0, 3))
    block = lax.all_to_all(local, "inp", split_axis=0, concat_axis=0, tiled=True)
    inputs = block.shape[0] * width
    blocks = lax.axis_size("tm")
    own = lax.axis_index("tm").astype(jnp.int32).reshape(1)
    spectra, vis = correlate(block, own, inputs // blocks, 1.0 / (frames * blocks))
    return (spectra[:, :, None], vis[:, None])


def solution(mesh):
    in_specs = (P(None, "tm", "inp"), P())
    out_specs = (P(None, "tm", ("freq", "inp"), None), P(None, ("freq", "inp"), "tm", None))
    return jax.shard_map(body, mesh=mesh, in_specs=in_specs, out_specs=out_specs, check_vma=False)
```

```python
import functools
import math

import jax
import jax.numpy as jnp
import numpy as np
from jax import lax
from jax.experimental import pallas as pl
from jax.experimental.pallas import tpu as pltpu
from jax.sharding import PartitionSpec as P

VM = pl.BlockSpec(memory_space=pltpu.VMEM)
SM = pl.BlockSpec(memory_space=pltpu.SMEM)
HB = pl.BlockSpec(memory_space=pltpu.HBM)
LOAD_LIMIT = 50 << 20
PARAMS = pltpu.CompilerParams(vmem_limit_bytes=16 << 20)


def from_behind(value):
    count, groups = lax.axis_size("tm"), lax.axis_size("freq")
    pairs = [
        (t * groups + (f ^ (groups // 2)), (t + 1) * groups + f)
        for t in range(count - 1)
        for f in range(groups)
    ]
    return lax.ppermute(value, ("tm", "freq"), pairs)


def tm_shift(value, dy, dx):
    ny = lax.axis_size("tm") // 2
    pairs = [
        (y * 2 + h, (y - dy) % ny * 2 + (h + dx) % 2) for y in range(ny) for h in range(2)
    ]
    return lax.ppermute(value, "tm", pairs)


def shares_of(taps, table_ref, frames):
    rows = table_ref.shape[0] // (2 * taps)
    width = frames[0][0].shape[1]
    x = jnp.concatenate([jnp.concatenate([p[0], p[1]], axis=0) for p in frames], axis=1)
    y = jnp.dot(table_ref[...], x, preferred_element_type=jnp.float32)
    parts = []
    for j in range(taps):
        at = 2 * j * rows
        parts.append(y[at : at + rows] + y[at + rows : at + 2 * rows])
    return [[part[:, s * width : (s + 1) * width] for part in parts] for s in range(len(frames))]


def advance(carry, share):
    sums = [c + s for c, s in zip(carry, share)] + [share[-1]]
    return sums[0], tuple(sums[1:])


def load_kernel(volt_ref, tail_ref, held_ref, sems):
    chunks = sems.shape[0] - 1
    samples = volt_ref.shape[1]
    span = samples // chunks
    last = tail_ref.shape[1]
    copies = [pltpu.make_async_copy(volt_ref.at[:, samples - last :], tail_ref, sems.at[chunks])]
    for i in range(chunks):
        part = slice(i * span, (i + 1) * span)
        copies.append(pltpu.make_async_copy(volt_ref.at[:, part], held_ref.at[:, part], sems.at[i]))
    for copy in copies:
        copy.start()
    for copy in copies:
        copy.wait()


def load(volt, last):
    return pl.pallas_call(
        load_kernel,
        out_shape=(
            jax.ShapeDtypeStruct((volt.shape[0], last, volt.shape[2]), volt.dtype),
            jax.ShapeDtypeStruct(volt.shape, volt.dtype),
        ),
        in_specs=[HB],
        out_specs=(VM, VM),
        scratch_shapes=[pltpu.SemaphoreType.DMA((5,))],
        cost_estimate=pl.CostEstimate(flops=0, bytes_accessed=4 * volt.size, transcendentals=0),
        compiler_params=pltpu.CompilerParams(vmem_limit_bytes=LOAD_LIMIT),
        name="load",
    )(volt)


def main_kernel(taps, _, table_ref, window_ref, volt_ref, out_ref, open_ref, split_ref):
    frames, rows, width = out_ref.shape
    chans = volt_ref.shape[1] // frames
    halo = taps - 1
    step = 16

    def frame_of(f):
        at = f * chans if isinstance(f, int) else pl.multiple_of(f * chans, chans)
        return [volt_ref[p, pl.ds(at, chans), :] for p in range(2)]

    base = table_ref[...]
    for j in range(taps):
        weights = window_ref[j : j + 1, :]
        tapped = base * jnp.concatenate([weights, weights], axis=1)
        coarse = tapped.astype(jnp.bfloat16)
        at = 2 * j * rows
        split_ref[at : at + rows, :] = coarse
        split_ref[at + rows : at + 2 * rows, :] = (tapped - coarse.astype(jnp.float32)).astype(jnp.bfloat16)

    def block(i, carry):
        every = []
        for s in range(0, step, 2):
            every += shares_of(taps, split_ref, [frame_of(i * step + s), frame_of(i * step + s + 1)])
        for s, share in enumerate(every):
            done, carry = advance(carry, share)
            out_ref[i * step + s] = done.astype(out_ref.dtype)
            if isinstance(i, int) and s < halo:
                open_ref[s] = done
        return carry

    carry = block(0, tuple(jnp.zeros((rows, width), jnp.float32) for _ in range(halo)))
    lax.fori_loop(1, frames // step, block, carry)


def head_kernel(taps, table_ref, prior_ref, open_ref, main_ref, out_ref):
    rows, width = out_ref.shape[1:]
    halo = taps - 1
    chans = prior_ref.shape[1] // halo
    frames = [[prior_ref[p, f * chans : (f + 1) * chans, :] for p in range(2)] for f in range(halo)]
    carry = tuple(jnp.zeros((rows, width), jnp.float32) for _ in range(halo))
    for share in shares_of(taps, table_ref, frames):
        _, carry = advance(carry, share)
    for f in range(halo):
        out_ref[f] = (open_ref[f] + carry[f]).astype(out_ref.dtype)


def dft_table(chans, group_size):
    channel = np.arange(chans).reshape(-1, group_size)
    phase = channel[:, :, None] * np.arange(chans) % chans * (2.0 * math.pi / chans)
    cosine = np.cos(phase) / math.sqrt(chans)
    sine = np.sin(phase) / math.sqrt(chans)
    real = np.concatenate([cosine, sine], axis=2)
    imag = np.concatenate([-sine, cosine], axis=2)
    return np.concatenate([real, imag], axis=1).astype(np.float32)


def channelize(held, prior, window, group, groups, frames):
    taps, chans = window.shape
    rows = 2 * chans // groups
    width = held.shape[2]
    table = jnp.asarray(dft_table(chans, chans // groups))
    local, open_sums, split = pl.pallas_call(
        functools.partial(main_kernel, taps),
        out_shape=(
            jax.ShapeDtypeStruct((frames, rows, width), jnp.bfloat16),
            jax.ShapeDtypeStruct((taps - 1, rows, width), jnp.float32),
            jax.ShapeDtypeStruct((taps * 2 * rows, 2 * chans), jnp.bfloat16),
        ),
        grid_spec=pltpu.PrefetchScalarGridSpec(
            num_scalar_prefetch=1,
            grid=(1,),
            in_specs=[
                pl.BlockSpec((None, rows, 2 * chans), lambda i, group: (group[0], 0, 0)),
                VM,
                VM,
            ],
            out_specs=(VM, VM, VM),
        ),
        cost_estimate=pl.CostEstimate(
            flops=4 * rows * taps * held.size, bytes_accessed=3 * held.size, transcendentals=0
        ),
        compiler_params=PARAMS,
        name="channelize",
    )(group, table, window, held)
    return pl.pallas_call(
        functools.partial(head_kernel, taps),
        out_shape=jax.ShapeDtypeStruct(local.shape, local.dtype),
        in_specs=[VM] * 4,
        out_specs=VM,
        input_output_aliases={3: 0},
        cost_estimate=pl.CostEstimate(
            flops=4 * rows * taps * prior.size, bytes_accessed=3 * prior.size, transcendentals=0
        ),
        compiler_params=PARAMS,
        name="channelize_head",
    )(split, prior, open_sums, local)


def fill_left(left_ref, at, piece, first, parts):
    blocks = [piece[first + s] for s in range(parts)]
    rows = jnp.concatenate([jnp.concatenate([b[0], b[1]], axis=0) for b in blocks], axis=1)
    turned = jnp.concatenate([jnp.concatenate([-b[1], b[0]], axis=0) for b in blocks], axis=1)
    both = jnp.concatenate([rows, turned], axis=1)
    left_ref[:, at : at + both.shape[0]] = both.T


def column_tile(pieces, z, wide):
    tall = []
    for piece in pieces:
        across = [piece[z + s] for s in range(wide)]
        across = [jnp.concatenate([b[0], b[1]], axis=0) for b in across]
        tall.append(jnp.concatenate(across, axis=1))
    return jnp.concatenate(tall, axis=0)


def spectra_kernel(block_ref, spectra_ref, token_ref, sems):
    token_ref[...] = jnp.zeros_like(token_ref)
    zs, _, _, width = block_ref.shape
    copies = []
    for z in range(zs):
        cols = slice(z * width, (z + 1) * width)
        copies.append(pltpu.make_async_copy(block_ref.at[z], spectra_ref.at[:, :, cols], sems.at[z]))
        copies[-1].start()
    for copy in copies:
        copy.wait()


def first_kernel(wide, own_ref, *refs):
    *pieces, total_ref, left_ref = refs
    zs, _, frames, width = pieces[0].shape
    parts = left_ref.shape[0] // (2 * width)
    for i, piece in enumerate(pieces):
        fill_left(left_ref, 2 * frames * i, piece, own_ref[0] * parts, parts)
    for z in range(0, zs, wide):
        total_ref[:, z * width : (z + wide) * width] = jnp.dot(
            left_ref[...], column_tile(pieces, z, wide), preferred_element_type=jnp.float32
        )


def more_kernel(wide, own_ref, before_ref, *refs):
    *pieces, total_ref, left_ref = refs
    zs, _, frames, width = pieces[0].shape
    parts = left_ref.shape[0] // (2 * width)
    for i, piece in enumerate(pieces):
        fill_left(left_ref, 2 * frames * i, piece, own_ref[0] * parts, parts)
    for z in range(0, zs, wide):
        cols = slice(z * width, (z + wide) * width)
        total_ref[:, cols] = before_ref[:, cols] + jnp.dot(
            left_ref[...], column_tile(pieces, z, wide), preferred_element_type=jnp.float32
        )


def last_kernel(wide, scale, own_ref, total_ref, low_ref, high_ref, vis_ref, left_ref, out_ref, sems):
    cut, _, frames, width = low_ref.shape
    zs = cut + high_ref.shape[0]
    rows = out_ref.shape[1]
    parts = rows // width
    first = own_ref[0] * parts

    @pl.when(first < cut)
    def _():
        fill_left(left_ref, 0, low_ref, first, parts)

    @pl.when(first >= cut)
    def _():
        fill_left(left_ref, 0, high_ref, first - cut, parts)

    copies = []
    for i, z in enumerate(range(0, zs, wide)):
        piece, at = (low_ref, z) if z < cut else (high_ref, z - cut)
        cols = slice(z * width, (z + wide) * width)
        product = jnp.dot(
            left_ref[...], column_tile([piece], at, wide), preferred_element_type=jnp.float32
        )
        out = ((product + total_ref[:, cols]) * scale).astype(out_ref.dtype)
        out_ref[0, :, cols] = out[:rows]
        out_ref[1, :, cols] = out[rows:]
        copies.append(
            pltpu.make_async_copy(out_ref.at[:, :, cols], vis_ref.at[:, :, cols], sems.at[i])
        )
        copies[-1].start()
    for copy in copies:
        copy.wait()


def spectra_of(block):
    zs, _, frames, width = block.shape
    return pl.pallas_call(
        spectra_kernel,
        out_shape=(
            jax.ShapeDtypeStruct((2, frames, zs * width), jnp.bfloat16),
            jax.ShapeDtypeStruct((8, 128), jnp.float32),
        ),
        in_specs=[VM],
        out_specs=(HB, VM),
        scratch_shapes=[pltpu.SemaphoreType.DMA((zs,))],
        cost_estimate=pl.CostEstimate(flops=0, bytes_accessed=4 * block.size, transcendentals=0),
        compiler_params=PARAMS,
        name="spectra_out",
    )(block)


def vis_first(own, pieces, rows):
    zs, _, frames, width = pieces[0].shape
    cols = zs * width
    depth = 2 * frames * len(pieces)
    return pl.pallas_call(
        functools.partial(first_kernel, 2),
        out_shape=jax.ShapeDtypeStruct((2 * rows, cols), jnp.float32),
        in_specs=[SM] + [VM] * len(pieces),
        out_specs=VM,
        scratch_shapes=[pltpu.VMEM((2 * rows, depth), jnp.bfloat16)],
        cost_estimate=pl.CostEstimate(
            flops=4 * rows * cols * depth, bytes_accessed=8 * rows * cols, transcendentals=0
        ),
        compiler_params=PARAMS,
        name="vis_first",
    )(own, *pieces)


def vis_more(own, total, pieces, rows):
    zs, _, frames, width = pieces[0].shape
    cols = zs * width
    depth = 2 * frames * len(pieces)
    return pl.pallas_call(
        functools.partial(more_kernel, 2),
        out_shape=jax.ShapeDtypeStruct((2 * rows, cols), jnp.float32),
        in_specs=[SM, VM] + [VM] * len(pieces),
        out_specs=VM,
        scratch_shapes=[pltpu.VMEM((2 * rows, depth), jnp.bfloat16)],
        input_output_aliases={1: 0},
        cost_estimate=pl.CostEstimate(
            flops=4 * rows * cols * depth, bytes_accessed=8 * rows * cols, transcendentals=0
        ),
        compiler_params=PARAMS,
        name="vis_more",
    )(own, total, *pieces)


def vis_last(own, total, low, high, rows, scale):
    frames, width = low.shape[2:]
    zs = low.shape[0] + high.shape[0]
    cols = zs * width
    wide = 2
    return pl.pallas_call(
        functools.partial(last_kernel, wide, scale),
        out_shape=jax.ShapeDtypeStruct((2, rows, cols), jnp.bfloat16),
        in_specs=[SM, VM, VM, VM],
        out_specs=HB,
        scratch_shapes=[
            pltpu.VMEM((2 * rows, 2 * frames), jnp.bfloat16),
            pltpu.VMEM((2, rows, cols), jnp.bfloat16),
            pltpu.SemaphoreType.DMA((zs // wide,)),
        ],
        cost_estimate=pl.CostEstimate(
            flops=8 * rows * cols * frames, bytes_accessed=8 * rows * cols, transcendentals=0
        ),
        compiler_params=PARAMS,
        name="vis_last",
    )(own, total, low, high)


def after_kernel(*refs):
    pass


def after(other, *values):
    count = len(values)
    return pl.pallas_call(
        after_kernel,
        out_shape=tuple(jax.ShapeDtypeStruct(v.shape, v.dtype) for v in values),
        in_specs=[VM] * count + [pl.BlockSpec(memory_space=pl.ANY)],
        out_specs=(VM,) * count,
        input_output_aliases={i: i for i in range(count)},
        compiler_params=PARAMS,
        name="after",
    )(*values, other)


def correlate(block, own, rows, scale):
    cut = block.shape[0] * 4 // 16 * 2
    up = tm_shift(block, 1, 0)
    across = tm_shift(block, 0, 1)
    down = tm_shift(block, -1, 0)
    spectra, written = spectra_of(block)
    (up,) = after(written, up)
    far = tm_shift(up, 1, 0)
    across_up = tm_shift(up, 0, 1)
    across, down = after(written, across, down)
    across_down = tm_shift(across, -1, 0)
    total = vis_first(own, [block, up, across, down], rows)
    (far,) = after(total, far)
    last_low = tm_shift(far[:cut], 0, 1)
    last_high = tm_shift(across_up[cut:], 1, 0)
    total = vis_more(own, total, [far, across_up, across_down], rows)
    return spectra, vis_last(own, total, last_low, last_high, rows, scale)


def body(volt, window):
    taps, chans = window.shape
    samples, width = volt.shape[1:]
    frames = samples // chans
    tail, held = load(volt, (taps - 1) * chans)
    prior = from_behind(tail)
    groups = lax.axis_size("freq")
    group = lax.axis_index("freq").astype(jnp.int32).reshape(1)
    local = channelize(held, prior, window, group, groups, frames)
    local = jnp.transpose(local.reshape(frames, 2, chans // groups, width), (2, 1, 0, 3))
    block = lax.all_to_all(local, "inp", split_axis=0, concat_axis=0, tiled=True)
    inputs = block.shape[0] * width
    blocks = lax.axis_size("tm")
    own = lax.axis_index("tm").astype(jnp.int32).reshape(1)
    spectra, vis = correlate(block, own, inputs // blocks, 1.0 / (frames * blocks))
    return (spectra[:, :, None], vis[:, None])


def solution(mesh):
    in_specs = (P(None, "tm", "inp"), P())
    out_specs = (P(None, "tm", ("freq", "inp"), None), P(None, ("freq", "inp"), "tm", None))
    return jax.shard_map(body, mesh=mesh, in_specs=in_specs, out_specs=out_specs, check_vma=False)
```
